768 devices in a mesh: dom: 192 (over y, z, core), sub: 4 (over x).
Axes of the slice: x: 4, y: 8, z: 12, core: 2. Of those that a mesh axis runs over, the one named last changes fastest.
Arguments:
- start_vector: float32 [192, 4, 16, 128], P('dom', 'sub')
- blocks: bfloat16 [192, 4, 16, 7, 128, 128], P('dom', 'sub')
- columns: int32 [192, 4, 16, 7], P('dom', 'sub'), may hold values from 0 to 143, as said below
- shifts: float32 [8], replicated, may hold values from 1.2 to 1.8
Outputs:
- basis: float32 [9, 192, 4, 16, 128], P(None, 'dom', 'sub')
- factor: float32 [9, 9], replicated
The draws below stay inside these ranges and needn't reach their ends.
Inputs may be any that keep to these rules, and one draw needn't show every extreme that they name: `columns`: entry 0 of block row r is the block row itself, slot 64 + r; other entries name any slot of the neighbourhood, repeats allowed.
All inputs are finite; a program needn't handle non-finite values.
Results may differ from the reference program's by a relative error of at most 0.0059.
Values may be sent and summed in bfloat16 or wider, within the bound.
No kernel may reach another device: no remote copies, remote signals or barrier semaphores. Data moves between devices by JAX's collectives and lax.ppermute only.
A program may use at most 32 MiB of HBM per device.

```python
import jax
import jax.numpy as jnp
from jax import lax

BLK = 128
BR = 16
NB = 7
S = 8
S1 = 9
DOMS = 192
SUBS = 4
ROWS = 1572864


def draw_start_vector(key, part):
    key = jax.random.fold_in(key, 11)
    ramp = 1.0 + 2.0 * jnp.arange(DOMS, dtype=jnp.float32) / (DOMS - 1)
    ramp = ramp.reshape(DOMS, 1, 1, 1)
    values = jax.random.normal(key, (DOMS, SUBS, BR, BLK), jnp.float32)
    return values * ramp


def draw_blocks(key, part):
    key = jax.random.fold_in(key, 23)
    noise_key, diag_key = jax.random.split(key)
    noise = jax.random.normal(noise_key, (DOMS, SUBS, BR, NB, BLK, BLK), jnp.float32)
    first = (jnp.arange(NB) == 0).reshape(1, 1, 1, NB, 1, 1)
    scale = jnp.where(first, 0.3 / BLK ** 0.5, 0.5 / (BLK * (NB - 1)) ** 0.5)
    diag_vals = jnp.exp(jax.random.uniform(diag_key, (DOMS, SUBS, BR, 1, BLK, 1), jnp.float32, 0.0, 0.6931))
    identity = jnp.eye(BLK, dtype=jnp.float32).reshape(1, 1, 1, 1, BLK, BLK)
    return (noise * scale + jnp.where(first, diag_vals * identity, 0.0)).astype(jnp.bfloat16)


def draw_columns(key, part):
    key = jax.random.fold_in(key, 37)
    slots = jax.random.randint(key, (DOMS, SUBS, BR, NB), 0, 9 * BR)
    rows = jnp.arange(BR, dtype=jnp.int32).reshape(1, 1, BR)
    slots = slots.at[:, :, :, 0].set(4 * BR + rows)
    slots = slots.at[:, :, 0, 1].set(9 * BR - 1)
    slots = slots.at[:, :, 1, 1].set(0)
    return slots.astype(jnp.int32)


def setup_inputs(seed: int = 0) -> dict:
    keys = jax.random.split(jax.random.key(seed), 5)
    start_vector = draw_start_vector(jax.random.fold_in(keys[4], 71), 0)
    blocks = draw_blocks(jax.random.fold_in(keys[4], 71), 0)
    columns = draw_columns(jax.random.fold_in(keys[4], 71), 0)
    shifts = jnp.clip(jax.random.uniform(keys[3], (S,), jnp.float32, 1.2, 1.8), 1.2, 1.8)
    return dict(start_vector=start_vector, blocks=blocks, columns=columns, shifts=shifts)


def apply_matrix(field, blocks, columns):
    padded = jnp.pad(field, ((1, 1), (1, 1), (0, 0), (0, 0)))
    slabs = [padded[a:a + DOMS, b:b + SUBS] for a in range(3) for b in range(3)]
    pool = jnp.stack(slabs, axis=2).reshape(DOMS, SUBS, 9 * BR, BLK)

    def one_domain(inputs):
        pool_dom, block_dom, column_dom = inputs
        slot_ids = column_dom.reshape(SUBS, BR * NB, 1).astype(jnp.int32)
        picked = jnp.take_along_axis(pool_dom, slot_ids, axis=1)
        picked = picked.reshape(SUBS, BR, NB, BLK).astype(jnp.bfloat16).astype(jnp.float32)
        return jnp.einsum('srnij,srnj->sri', block_dom.astype(jnp.float32), picked)
    return lax.map(one_domain, (pool, blocks, columns))

def reference(start_vector, blocks, columns, shifts):
    vectors = [start_vector]
    for section in range(S):
        image = apply_matrix(vectors[-1], blocks, columns)
        vectors.append(image - shifts[section] * vectors[-1])
    basis = jnp.stack(vectors, axis=0)
    flat = basis.reshape(S1, -1)
    gram = jnp.dot(flat, flat.T, precision=lax.Precision.HIGHEST) / ROWS
    factor = jnp.linalg.cholesky(gram).T
    return (basis, factor)
```

```python
import functools

import jax
import jax.numpy as jnp
from jax import lax
from jax.experimental import pallas as pl
from jax.experimental.pallas import tpu as pltpu
from jax.sharding import Mesh, PartitionSpec as P

S = 8
S1 = 9
NB = 7
BR = 16
BLK = 128
SUBS = 4
NY, NZ, NCORE = 8, 12, 2
DOMS = NY * NZ * NCORE
CHIPS = DOMS // NCORE
DOM = ("y", "z", "core")
ALL = DOM + ("sub",)
VMEM = pl.BlockSpec(memory_space=pltpu.VMEM)
PARAMS = pltpu.CompilerParams(vmem_limit_bytes=16 * 1024 * 1024)


def outer_groups():
    return [
        [(d % DOMS) * SUBS + s for d in (2 * c - 1, 2 * c) for s in range(SUBS)]
        for c in range(CHIPS)
    ]


def pool_rows(columns):
    d = (lax.axis_index("y") * NZ + lax.axis_index("z")) * NCORE + lax.axis_index("core")
    s = lax.axis_index("sub")
    core = lax.axis_index("core")
    slot, row = columns // BR, columns % BR
    a, b = slot // 3 - 1, slot % 3 - 1
    chip_core = core + a
    member = jnp.where(core == 0, jnp.where(a < 0, 0, 1), jnp.where(a > 0, 1, 0))
    held = chip_core % NCORE
    nd, ns = d + a, s + b
    inside = (nd >= 0) & (nd < DOMS) & (ns >= 0) & (ns < SUBS)
    index = ((member * SUBS + ns) * NCORE + held) * BR + row
    return jnp.where(inside, index, -1)


def product(k, pool_ref, hot_ref, blocks_ref, v_ref, shifts_ref):
    pool = pool_ref[...].reshape(-1, BLK)
    picked = jnp.dot(hot_ref[...], pool, preferred_element_type=jnp.float32).astype(jnp.bfloat16)
    parts = [picked[n * BR:(n + 1) * BR] for n in range(NB)]
    wide = [jnp.concatenate(parts[n:n + 2], axis=1) for n in range(0, NB, 2)]
    lane = lax.broadcasted_iota(jnp.int32, (BR, BLK), 0)
    total = jnp.zeros((BR, BLK), jnp.float32)
    for r in range(BR):
        acc = None
        for p, x in enumerate(wide):
            rows = [blocks_ref[r, n] for n in range(2 * p, min(2 * p + 2, NB))]
            block = jnp.concatenate(rows, axis=1)
            term = lax.dot_general(x, block, (((1,), (1,)), ((), ())), preferred_element_type=jnp.float32)
            acc = term if acc is None else acc + term
        total = jnp.where(lane == r, acc, total)
    return total - shifts_ref[0:1, k:k + 1] * v_ref[...]


def step_kernel(k, pool_ref, hot_ref, blocks_ref, v_ref, shifts_ref, out_ref, rounded_ref):
    new = product(k, pool_ref, hot_ref, blocks_ref, v_ref, shifts_ref)
    out_ref[...] = new
    rounded_ref[...] = new.astype(jnp.bfloat16)


def last_kernel(pool_ref, hot_ref, blocks_ref, shifts_ref, *refs):
    ins, basis_ref, gram_ref = refs[:S], refs[S], refs[S + 1]
    vectors = [ref[...] for ref in ins]
    new = product(S - 1, pool_ref, hot_ref, blocks_ref, ins[-1], shifts_ref)
    vectors.append(new)
    for i, v in enumerate(vectors):
        basis_ref[i] = v
    lane = lax.broadcasted_iota(jnp.int32, (S, BLK), 1)
    sub = lax.broadcasted_iota(jnp.int32, (S, BLK), 0)
    tile = jnp.zeros((S, BLK), jnp.float32)

    def rows(i, j):
        prod = vectors[i] * vectors[j]
        return jnp.sum(prod, axis=0, keepdims=True)

    for i in range(S1):
        stack = jnp.zeros((S, BLK), jnp.float32)
        for j in range(min(i + 1, S)):
            stack = jnp.where(sub == j, rows(i, j), stack)
        tile = jnp.where(lane == i, jnp.sum(stack, axis=1, keepdims=True), tile)
    corner = jnp.sum(rows(S, S), axis=1, keepdims=True)
    gram_ref[...] = jnp.where((lane == S1) & (sub == 0), corner, tile)


def factor_kernel(rows_total, parts_ref, out_ref):
    tile = jnp.sum(parts_ref[...], axis=0) / rows_total
    size = 16
    pad = jnp.concatenate([tile, jnp.zeros((size - S, BLK), jnp.float32)], axis=0)
    lane = lax.broadcasted_iota(jnp.int32, (size, BLK), 1)
    sub = lax.broadcasted_iota(jnp.int32, (size, BLK), 0)
    upper = jnp.where((sub == S) & (lane == S), pad[0:1, S1:S1 + 1], jnp.where((lane >= sub) & (lane < S1), pad, 0.0))
    full = upper
    result = jnp.zeros((size, BLK), jnp.float32)
    for k in range(S1):
        row = full[k:k + 1, :]
        pivot = row[:, k:k + 1]
        root = jnp.sqrt(pivot)
        line = jnp.where(lane[0:1] >= k, row, 0.0) / root
        result = jnp.where(sub == k, line, result)
        spread = jnp.broadcast_to(line, (size, BLK))
        down = jnp.sum(jnp.where(lane == sub, spread, 0.0), axis=1, keepdims=True)
        full = full - down * line
    out_ref[...] = result[0:S1, 0:S1]


def step(k, pool, hot, blocks, v, shifts):
    return pl.pallas_call(
        functools.partial(step_kernel, k),
        out_shape=(jax.ShapeDtypeStruct((BR, BLK), jnp.float32), jax.ShapeDtypeStruct((BR, BLK), jnp.bfloat16)),
        in_specs=[VMEM] * 5,
        out_specs=(VMEM, VMEM),
        compiler_params=PARAMS,
        name="step",
    )(pool, hot, blocks, v, shifts)


def last_step(pool, hot, blocks, shifts, vectors):
    return pl.pallas_call(
        last_kernel,
        out_shape=(jax.ShapeDtypeStruct((S1, BR, BLK), jnp.float32), jax.ShapeDtypeStruct((S, BLK), jnp.float32)),
        in_specs=[VMEM] * (4 + S),
        out_specs=(VMEM, VMEM),
        compiler_params=PARAMS,
        name="last",
    )(pool, hot, blocks, shifts, *vectors)


def to_all(value, axes, peers):
    return lax.all_to_all(jnp.broadcast_to(value, (peers,) + value.shape), axes, 0, 0)


def on_device(groups, start_vector, blocks, columns, shifts):
    blocks = blocks[0, 0]
    rows = pool_rows(columns[0, 0]).T.reshape(NB * BR, 1)
    pool_size = len(groups[0]) * NCORE * BR
    hot = (rows == lax.broadcasted_iota(jnp.int32, (NB * BR, pool_size), 1)).astype(jnp.bfloat16)
    shifts = shifts.reshape(1, S)
    v = start_vector[0, 0]
    rounded = v.astype(jnp.bfloat16)
    vectors = [v]
    for k in range(S):
        chip = lax.all_gather(rounded, "core")
        chip = jnp.broadcast_to(chip, (len(groups[0]),) + chip.shape)
        pool = lax.all_to_all(chip, ALL, 0, 0, axis_index_groups=groups)
        if k < S - 1:
            v, rounded = step(k, pool, hot, blocks, v, shifts)
            vectors.append(v)
    basis, gram = last_step(pool, hot, blocks, shifts, vectors)
    gram = jnp.sum(to_all(gram, ("y", "sub"), NY * SUBS), axis=0)
    parts = to_all(gram, ("z", "core"), NZ * NCORE)
    factor = pl.pallas_call(
        functools.partial(factor_kernel, DOMS * SUBS * BR * BLK),
        out_shape=jax.ShapeDtypeStruct((S1, S1), jnp.float32),
        in_specs=[VMEM],
        out_specs=VMEM,
        name="factor",
    )(parts)
    return basis.reshape(S1, 1, 1, BR, BLK), factor


def solution(mesh):
    split = Mesh(mesh.devices.reshape(NY, NZ, NCORE, SUBS), ALL)
    return jax.shard_map(
        functools.partial(on_device, outer_groups()),
        mesh=split,
        in_specs=(P(DOM, "sub"), P(DOM, "sub"), P(DOM, "sub"), P()),
        out_specs=(P(None, DOM, "sub"), P()),
        check_vma=False,
    )
```

```python
import functools

import jax
import jax.numpy as jnp
from jax import lax
from jax.experimental import pallas as pl
from jax.experimental.pallas import tpu as pltpu
from jax.sharding import Mesh, PartitionSpec as P

S = 8
S1 = 9
NB = 7
BR = 16
BLK = 128
MATRIX_ROWS = 6
SUBS = 4
NY, NZ, NCORE = 8, 12, 2
DOMS = NY * NZ * NCORE
CHIPS = DOMS // NCORE
PEERS = 2 * SUBS
POOL = PEERS * NCORE * BR
DOM = ("y", "z", "core")
ALL = DOM + ("sub",)
VMEM = pl.BlockSpec(memory_space=pltpu.VMEM)
PARAMS = pltpu.CompilerParams(vmem_limit_bytes=16 * 1024 * 1024)


def outer_groups():
    return [
        [(d % DOMS) * SUBS + s for d in (2 * c - 1, 2 * c) for s in range(SUBS)]
        for c in range(CHIPS)
    ]


def pool_rows(columns):
    core, s = lax.axis_index("core"), lax.axis_index("sub")
    d = (lax.axis_index("y") * NZ + lax.axis_index("z")) * NCORE + core
    slot, row = columns // BR, columns % BR
    a, b = slot // 3 - 1, slot % 3 - 1
    member = jnp.where((a < 0) & (core == 0), 0, jnp.where((a > 0) | (core == 0), 1, 0))
    held = (core + a + NCORE) % NCORE
    nd, ns = d + a, s + b
    inside = (nd >= 0) & (nd < DOMS) & (ns >= 0) & (ns < SUBS)
    index = ((member * SUBS + ns) * NCORE + held) * BR + row
    return jnp.where(inside, index, -1)


def one_hot(columns):
    rows = pool_rows(columns)
    place = lax.broadcasted_iota(jnp.int32, (BR, POOL), 1)
    return jnp.concatenate(
        [jnp.where(rows[:, n:n + 1] == place, 1.0, 0.0) for n in range(NB)], axis=0
    ).astype(jnp.bfloat16)


def product(k, pool_ref, hot_ref, blocks_ref, v_ref, packed_ref):
    pool = pool_ref[...].reshape(POOL, BLK)
    picked = jnp.dot(hot_ref[...], pool, preferred_element_type=jnp.float32)
    fields = [picked[n * BR:(n + 1) * BR] for n in range(NB)]
    line = jnp.concatenate(fields, axis=1).astype(jnp.bfloat16)
    row = lax.broadcasted_iota(jnp.int32, (BR, BLK), 0)
    lane = lax.broadcasted_iota(jnp.int32, (BLK, BLK), 1)
    by_matrix = jnp.zeros((BR, BLK), jnp.float32)
    by_vector = jnp.zeros((BLK, BLK), jnp.float32)

    def matrix_unit(r, total):
        block = jnp.concatenate([blocks_ref[r:r + 2, n].reshape(2 * BLK, BLK) for n in range(NB)], axis=1)
        pair = lax.dot_general(line, block, (((1,), (1,)), ((), ())), preferred_element_type=jnp.float32)
        return jnp.where(row == r, pair[:, :BLK], jnp.where(row == r + 1, pair[:, BLK:], total))

    def vector_unit(r, total):
        acc = None
        for n in range(NB):
            term = blocks_ref[r, n].astype(jnp.float32) * fields[n][r:r + 1]
            acc = term if acc is None else acc + term
        return jnp.where(lane == r, jnp.sum(acc, axis=1, keepdims=True), total)

    pairs, singles = list(range(0, MATRIX_ROWS, 2)), list(range(MATRIX_ROWS, BR))
    while pairs or singles:
        if pairs:
            by_matrix = matrix_unit(pairs.pop(0), by_matrix)
        if singles:
            by_vector = vector_unit(singles.pop(0), by_vector)
    image = jnp.where(row < MATRIX_ROWS, by_matrix, by_vector.T[:BR])
    return image - packed_ref[2 * BR:2 * BR + 1, k:k + 1] * v_ref[0:BR, :]


def spread_kernel(both_ref, packed_ref, blocks_ref, out_ref, hot_ref):
    both = both_ref[:, 0:BR, :].astype(jnp.bfloat16)
    for i in range(PEERS):
        out_ref[i] = both
    hot_ref[...] = one_hot(packed_ref[BR:2 * BR, :].astype(jnp.int32))


def step_kernel(k, pool_ref, hot_ref, blocks_ref, v_ref, packed_ref, out_ref, rounded_ref):
    new = product(k, pool_ref, hot_ref, blocks_ref, v_ref, packed_ref)
    out_ref[...] = new
    rounded_ref[...] = new.astype(jnp.bfloat16)


def inner(v, others):
    sub = lax.broadcasted_iota(jnp.int32, (S, BLK), 0)
    stack = jnp.zeros((S, BLK), jnp.float32)
    for j, w in enumerate(others):
        stack = jnp.where(sub == j, jnp.sum(v * w, axis=0, keepdims=True), stack)
    return jnp.sum(stack, axis=1, keepdims=True)


def last_kernel(pool_ref, hot_ref, blocks_ref, packed_ref, *refs):
    ins, out_ref, gram_ref = refs[:S], refs[S], refs[S + 1]
    new = product(S - 1, pool_ref, hot_ref, blocks_ref, ins[-1], packed_ref)
    out_ref[...] = new
    vectors = [ref[0:BR, :] for ref in ins] + [new]
    lane = lax.broadcasted_iota(jnp.int32, (S, BLK), 1)
    tile = jnp.zeros((S, BLK), jnp.float32)
    for i in range(S1):
        tile = jnp.where(lane == i, inner(vectors[i], vectors[:min(i + 1, S)]), tile)
    gram_ref[...] = jnp.where(lane == S1, inner(new, [new]), tile)


def factor_kernel(rows_total, parts_ref, *refs):
    out_ref, basis_ref = refs[S1], refs[S1 + 1]
    for i in range(S1):
        basis_ref[i] = refs[i][0:BR, :]
    tile = jnp.sum(parts_ref[...], axis=0) / rows_total
    spread = [jnp.broadcast_to(tile[:, i:i + 1], (S, BLK)) for i in range(S1 + 1)]
    a = {(j, i): jnp.broadcast_to(spread[i][j:j + 1], (S, BLK)) for i in range(S1) for j in range(min(i + 1, S))}
    a[S, S] = jnp.broadcast_to(spread[S1][0:1], (S, BLK))
    sub = lax.broadcasted_iota(jnp.int32, (S, BLK), 0)
    lane = lax.broadcasted_iota(jnp.int32, (S, BLK), 1)
    top = jnp.zeros((S, BLK), jnp.float32)
    bottom = None
    for k in range(S1):
        scale = lax.rsqrt(a[k, k])
        r = [a[k, i] * scale for i in range(k, S1)]
        whole = jnp.zeros((S, BLK), jnp.float32)
        for i in range(k, S1):
            whole = jnp.where(lane == i, r[i - k], whole)
            for j in range(k + 1, i + 1):
                a[j, i] = a[j, i] - r[j - k] * r[i - k]
        if k < S:
            top = jnp.where(sub == k, whole, top)
        else:
            bottom = whole
    out_ref[0:S, :] = top[:, 0:S1]
    out_ref[S:S1, :] = bottom[0:1, 0:S1]


def shape(*dims, dtype=jnp.float32):
    return jax.ShapeDtypeStruct(dims, dtype)


def spread(both, packed, blocks):
    return pl.pallas_call(
        spread_kernel,
        out_shape=(
            shape(PEERS, NCORE, BR, BLK, dtype=jnp.bfloat16),
            shape(NB * BR, POOL, dtype=jnp.bfloat16),
        ),
        in_specs=[VMEM] * 3,
        out_specs=(VMEM,) * 2,
        compiler_params=PARAMS,
        name="spread",
    )(both, packed, blocks)


def step(k, pool, hot, blocks, v, packed):
    return pl.pallas_call(
        functools.partial(step_kernel, k),
        out_shape=(shape(BR, BLK), shape(BR, BLK, dtype=jnp.bfloat16)),
        in_specs=[VMEM] * 5,
        out_specs=(VMEM, VMEM),
        compiler_params=PARAMS,
        name="step",
    )(pool, hot, blocks, v, packed)


def last_step(pool, hot, blocks, packed, vectors):
    return pl.pallas_call(
        last_kernel,
        out_shape=(shape(BR, BLK), shape(S, BLK)),
        in_specs=[VMEM] * (4 + S),
        out_specs=(VMEM, VMEM),
        compiler_params=PARAMS,
        name="last",
    )(pool, hot, blocks, packed, *vectors)


def to_all(value, axes, peers):
    return lax.all_to_all(jnp.broadcast_to(value, (peers,) + value.shape), axes, 0, 0)


def on_device(groups, start_vector, blocks, columns, shifts):
    blocks = blocks[0, 0]
    packed = jnp.concatenate([
        start_vector[0, 0],
        jnp.pad(columns[0, 0].astype(jnp.float32), ((0, 0), (0, BLK - NB))),
        jnp.pad(shifts.reshape(1, S), ((0, 7), (0, BLK - S))),
    ], axis=0)
    vectors = [packed]
    for k in range(S):
        if k == 0:
            chip, hot = spread(lax.all_gather(packed, "core"), packed, blocks)
        else:
            chip = lax.all_gather(rounded, "core")
            chip = jnp.broadcast_to(chip, (PEERS,) + chip.shape)
        pool = lax.all_to_all(chip, ALL, 0, 0, axis_index_groups=groups)
        if k < S - 1:
            v, rounded = step(k, pool, hot, blocks, vectors[-1], packed)
            vectors.append(v)
    v, gram = last_step(pool, hot, blocks, packed, vectors)
    gram = jnp.sum(to_all(gram, ("y", "sub"), NY * SUBS), axis=0)
    parts = to_all(gram, ("z", "core"), NZ * NCORE)
    factor, basis = pl.pallas_call(
        functools.partial(factor_kernel, DOMS * SUBS * BR * BLK),
        out_shape=(shape(S1, S1), shape(S1, BR, BLK)),
        in_specs=[VMEM] * (S1 + 1),
        out_specs=(VMEM, VMEM),
        compiler_params=PARAMS,
        name="factor",
    )(parts, *vectors, v)
    return basis.reshape(S1, 1, 1, BR, BLK), factor


def solution(mesh):
    split = Mesh(mesh.devices.reshape(NY, NZ, NCORE, SUBS), ALL)
    return jax.shard_map(
        functools.partial(on_device, outer_groups()),
        mesh=split,
        in_specs=(P(DOM, "sub"), P(DOM, "sub"), P(DOM, "sub"), P()),
        out_specs=(P(None, DOM, "sub"), P()),
        check_vma=False,
    )
```

```python
import functools

import jax
import jax.numpy as jnp
from jax import lax
from jax.experimental import pallas as pl
from jax.experimental.pallas import tpu as pltpu
from jax.sharding import Mesh, PartitionSpec as P

S = 8
S1 = 9
NB = 7
BR = 16
BLK = 128
MATRIX_ROWS = 6
SUBS = 4
NY, NZ, NCORE = 8, 12, 2
DOMS = NY * NZ * NCORE
CHIPS = DOMS // NCORE
GAP = 16
PEERS = 2 * SUBS
POOL = PEERS * NCORE * BR
DOM = ("y", "z", "core")
ALL = DOM + ("sub",)
VMEM = pl.BlockSpec(memory_space=pltpu.VMEM)
PARAMS = pltpu.CompilerParams(vmem_limit_bytes=16 * 1024 * 1024)


def outer_groups():
    return [
        [(d % DOMS) * SUBS + s for d in (2 * c - 1, 2 * c) for s in range(SUBS)]
        for c in range(CHIPS)
    ]


def pool_rows(columns):
    core, s = lax.axis_index("core"), lax.axis_index("sub")
    d = (lax.axis_index("y") * NZ + lax.axis_index("z")) * NCORE + core
    slot, row = columns // BR, columns % BR
    a, b = slot // 3 - 1, slot % 3 - 1
    member = jnp.where((a < 0) & (core == 0), 0, jnp.where((a > 0) | (core == 0), 1, 0))
    held = (core + a + NCORE) % NCORE
    nd, ns = d + a, s + b
    inside = (nd >= 0) & (nd < DOMS) & (ns >= 0) & (ns < SUBS)
    index = ((member * SUBS + ns) * NCORE + held) * BR + row
    return jnp.where(inside, index, -1)


def one_hot(lines):
    place = lax.broadcasted_iota(jnp.int32, (BR, POOL), 1)
    own = lax.broadcasted_iota(jnp.int32, (BR, BLK), 0) == lax.broadcasted_iota(jnp.int32, (BR, BLK), 1)
    parts = []
    for line in lines:
        rows = pool_rows(line).astype(jnp.float32)
        down = jnp.sum(jnp.where(own, rows, 0.0), axis=1, keepdims=True).astype(jnp.int32)
        parts.append(jnp.where(down == place, 1.0, 0.0))
    return jnp.concatenate(parts, axis=0).astype(jnp.bfloat16)


def product(k, pool_ref, hot_ref, blocks_ref, v_ref, shifts_ref):
    pool = pool_ref[...].reshape(POOL, BLK)
    picked = jnp.dot(hot_ref[...], pool, preferred_element_type=jnp.float32)
    fields = [picked[n * BR:(n + 1) * BR] for n in range(NB)]
    line = jnp.concatenate(fields, axis=1).astype(jnp.bfloat16)
    row = lax.broadcasted_iota(jnp.int32, (BR, BLK), 0)
    lane = lax.broadcasted_iota(jnp.int32, (BLK, BLK), 1)
    by_matrix = jnp.zeros((BR, BLK), jnp.float32)
    by_vector = jnp.zeros((BLK, BLK), jnp.float32)

    def matrix_unit(r, total):
        block = jnp.concatenate([blocks_ref[r:r + 2, n].reshape(2 * BLK, BLK) for n in range(NB)], axis=1)
        pair = lax.dot_general(line, block, (((1,), (1,)), ((), ())), preferred_element_type=jnp.float32)
        return jnp.where(row == r, pair[:, :BLK], jnp.where(row == r + 1, pair[:, BLK:], total))

    def vector_unit(r, total):
        acc = None
        for n in range(NB):
            term = blocks_ref[r, n].astype(jnp.float32) * fields[n][r:r + 1]
            acc = term if acc is None else acc + term
        return jnp.where(lane == r, jnp.sum(acc, axis=1, keepdims=True), total)

    pairs, singles = list(range(0, MATRIX_ROWS, 2)), list(range(MATRIX_ROWS, BR))
    while pairs or singles:
        if pairs:
            by_matrix = matrix_unit(pairs.pop(0), by_matrix)
        if singles:
            by_vector = vector_unit(singles.pop(0), by_vector)
    image = jnp.where(row < MATRIX_ROWS, by_matrix, by_vector.T[:BR])
    return image - shifts_ref[0:1, k:k + 1] * v_ref[0:BR, :]


def spread_kernel(both_ref, *refs):
    out_ref = refs[-1]
    both = both_ref[...].astype(jnp.bfloat16)
    for i in range(PEERS):
        out_ref[i] = both


def first_kernel(pool_ref, columns_ref, blocks_ref, v_ref, shifts_ref, out_ref, rounded_ref, hot_ref):
    wide = jnp.zeros((1, BLK - BR), jnp.int32)
    hot_ref[...] = one_hot([jnp.concatenate([columns_ref[n], wide], axis=1) for n in range(NB)])
    step_kernel(0, pool_ref, hot_ref, blocks_ref, v_ref, shifts_ref, out_ref, rounded_ref)


def step_kernel(k, pool_ref, hot_ref, blocks_ref, v_ref, shifts_ref, out_ref, rounded_ref):
    new = product(k, pool_ref, hot_ref, blocks_ref, v_ref, shifts_ref)
    out_ref[...] = new
    rounded_ref[...] = new.astype(jnp.bfloat16)


def inner(v, others):
    sub = lax.broadcasted_iota(jnp.int32, (S, BLK), 0)
    stack = jnp.zeros((S, BLK), jnp.float32)
    for j, w in enumerate(others):
        stack = jnp.where(sub == j, jnp.sum(v * w, axis=0, keepdims=True), stack)
    return jnp.sum(stack, axis=1, keepdims=True)


def last_kernel(pool_ref, hot_ref, blocks_ref, shifts_ref, *refs):
    ins, out_ref, gram_ref = refs[:S], refs[S], refs[S + 1]
    new = product(S - 1, pool_ref, hot_ref, blocks_ref, ins[-1], shifts_ref)
    out_ref[...] = new
    vectors = [ref[0:BR, :] for ref in ins] + [new]
    lane = lax.broadcasted_iota(jnp.int32, (S, BLK), 1) - GAP * lax.broadcasted_iota(jnp.int32, (S, BLK), 0)
    tile = jnp.zeros((S, BLK), jnp.float32)
    for i in range(S1):
        count = min(i + 1, S)
        tile = jnp.where((lane == i), inner(vectors[i], vectors[:count]), tile)
    row = jnp.sum(tile, axis=0, keepdims=True)
    place = lax.broadcasted_iota(jnp.int32, (1, BLK), 1)
    corner = jnp.sum(jnp.sum(new * new, axis=0, keepdims=True), axis=1, keepdims=True)
    gram_ref[...] = jnp.where(place == S1, corner, row)


def factor_kernel(rows_total, parts_ref, *refs):
    out_ref, basis_ref = refs[S1], refs[S1 + 1]
    for i in range(S1):
        basis_ref[i] = refs[i][0:BR, :]
    tile = jnp.broadcast_to(jnp.sum(parts_ref[...], axis=0) / rows_total, (S, BLK))

    def spread_lane(p):
        return jnp.broadcast_to(tile[:, p:p + 1], (S, BLK))

    a = {(j, i): spread_lane(GAP * j + i) for i in range(S1) for j in range(min(i + 1, S))}
    a[S, S] = spread_lane(S1)
    sub = lax.broadcasted_iota(jnp.int32, (S, BLK), 0)
    lane = lax.broadcasted_iota(jnp.int32, (S, BLK), 1)
    top = jnp.zeros((S, BLK), jnp.float32)
    bottom = None
    for k in range(S1):
        scale = lax.rsqrt(a[k, k])
        r = [a[k, i] * scale for i in range(k, S1)]
        whole = jnp.zeros((S, BLK), jnp.float32)
        for i in range(k, S1):
            whole = jnp.where(lane == i, r[i - k], whole)
            for j in range(k + 1, i + 1):
                a[j, i] = a[j, i] - r[j - k] * r[i - k]
        if k < S:
            top = jnp.where(sub == k, whole, top)
        else:
            bottom = whole
    out_ref[0:S, :] = top[:, 0:S1]
    out_ref[S:S1, :] = bottom[0:1, 0:S1]


def shape(*dims, dtype=jnp.float32):
    return jax.ShapeDtypeStruct(dims, dtype)


def spread(both, *others):
    return pl.pallas_call(
        spread_kernel,
        out_shape=shape(PEERS, NCORE, BR, BLK, dtype=jnp.bfloat16),
        in_specs=[VMEM] + [pl.BlockSpec(memory_space=pl.ANY)] * len(others),
        out_specs=VMEM,
        compiler_params=pltpu.CompilerParams(vmem_limit_bytes=58 * 1024 * 1024),
        name="spread",
    )(both, *others)


def first_step(pool, columns, blocks, v, shifts):
    return pl.pallas_call(
        first_kernel,
        out_shape=(
            shape(BR, BLK),
            shape(BR, BLK, dtype=jnp.bfloat16),
            shape(NB * BR, POOL, dtype=jnp.bfloat16),
        ),
        in_specs=[VMEM] * 5,
        out_specs=(VMEM,) * 3,
        compiler_params=PARAMS,
        name="first",
    )(pool, columns, blocks, v, shifts)


def step(k, pool, hot, blocks, v, shifts):
    return pl.pallas_call(
        functools.partial(step_kernel, k),
        out_shape=(shape(BR, BLK), shape(BR, BLK, dtype=jnp.bfloat16)),
        in_specs=[VMEM] * 5,
        out_specs=(VMEM, VMEM),
        compiler_params=PARAMS,
        name="step",
    )(pool, hot, blocks, v, shifts)


def last_step(pool, hot, blocks, shifts, vectors):
    return pl.pallas_call(
        last_kernel,
        out_shape=(shape(BR, BLK), shape(1, BLK)),
        in_specs=[VMEM] * (4 + S),
        out_specs=(VMEM, VMEM),
        compiler_params=PARAMS,
        name="last",
    )(pool, hot, blocks, shifts, *vectors)


def to_all(value, axes, peers):
    return lax.all_to_all(jnp.broadcast_to(value, (peers,) + value.shape), axes, 0, 0)


def on_device(groups, start_vector, blocks, columns, shifts):
    blocks = blocks[0, 0]
    columns = columns[0].transpose(2, 0, 1)
    shifts = shifts.reshape(1, S)
    v = start_vector[0, 0]
    vectors = [v]
    chip = spread(lax.all_gather(v, "core"), v, blocks, columns, shifts)
    for k in range(S):
        if k > 0:
            chip = lax.all_gather(rounded, "core")
            chip = jnp.broadcast_to(chip, (PEERS,) + chip.shape)
        pool = lax.all_to_all(chip, ALL, 0, 0, axis_index_groups=groups)
        if k == 0:
            v, rounded, hot = first_step(pool, columns, blocks, v, shifts)
        elif k < S - 1:
            v, rounded = step(k, pool, hot, blocks, v, shifts)
        if k < S - 1:
            vectors.append(v)
    v, gram = last_step(pool, hot, blocks, shifts, vectors)
    gram = jnp.sum(to_all(gram, ("y", "sub"), NY * SUBS), axis=0)
    parts = to_all(gram, ("z", "core"), NZ * NCORE)
    factor, basis = pl.pallas_call(
        functools.partial(factor_kernel, DOMS * SUBS * BR * BLK),
        out_shape=(shape(S1, S1), shape(S1, BR, BLK)),
        in_specs=[VMEM] * (S1 + 1),
        out_specs=(VMEM, VMEM),
        compiler_params=PARAMS,
        name="factor",
    )(parts, *vectors, v)
    return basis.reshape(S1, 1, 1, BR, BLK), factor


def solution(mesh):
    split = Mesh(mesh.devices.reshape(NY, NZ, NCORE, SUBS), ALL)
    return jax.shard_map(
        functools.partial(on_device, outer_groups()),
        mesh=split,
        in_specs=(P(DOM, "sub"), P(DOM, "sub"), P(DOM, "sub"), P()),
        out_specs=(P(None, DOM, "sub"), P()),
        check_vma=False,
    )
```

```python
import functools

import jax
import jax.numpy as jnp
from jax import lax
from jax.experimental import pallas as pl
from jax.experimental.pallas import tpu as pltpu
from jax.sharding import Mesh, PartitionSpec as P

S = 8
S1 = 9
NB = 7
BR = 16
BLK = 128
MATRIX_ROWS = 6
SUBS = 4
NY, NZ, NCORE = 8, 12, 2
DOMS = NY * NZ * NCORE
CHIPS = DOMS // NCORE
GAP = 16
PEERS = 2 * SUBS
POOL = PEERS * NCORE * BR
DOM = ("y", "z", "core")
ALL = DOM + ("sub",)
VMEM = pl.BlockSpec(memory_space=pltpu.VMEM)
PARAMS = pltpu.CompilerParams(vmem_limit_bytes=16 * 1024 * 1024)


def outer_groups():
    return [
        [(d % DOMS) * SUBS + s for d in (2 * c - 1, 2 * c) for s in range(SUBS)]
        for c in range(CHIPS)
    ]


def pool_rows(columns):
    core, s = lax.axis_index("core"), lax.axis_index("sub")
    d = (lax.axis_index("y") * NZ + lax.axis_index("z")) * NCORE + core
    slot, row = columns // BR, columns % BR
    a, b = slot // 3 - 1, slot % 3 - 1
    member = jnp.where((a < 0) & (core == 0), 0, jnp.where((a > 0) | (core == 0), 1, 0))
    held = (core + a + NCORE) % NCORE
    nd, ns = d + a, s + b
    inside = (nd >= 0) & (nd < DOMS) & (ns >= 0) & (ns < SUBS)
    index = ((member * SUBS + ns) * NCORE + held) * BR + row
    return jnp.where(inside, index, -1)


def one_hot(lines):
    place = lax.broadcasted_iota(jnp.int32, (BR, POOL), 1)
    own = lax.broadcasted_iota(jnp.int32, (BR, BLK), 0) == lax.broadcasted_iota(jnp.int32, (BR, BLK), 1)
    parts = []
    for line in lines:
        rows = pool_rows(line).astype(jnp.float32)
        down = jnp.sum(jnp.where(own, rows, 0.0), axis=1, keepdims=True).astype(jnp.int32)
        parts.append(jnp.where(down == place, 1.0, 0.0))
    return jnp.concatenate(parts, axis=0).astype(jnp.bfloat16)


def product(k, pool_ref, hot_ref, blocks_ref, v_ref, shifts_ref):
    pool = pool_ref[...].reshape(POOL, BLK)
    picked = jnp.dot(hot_ref[...], pool, preferred_element_type=jnp.float32)
    fields = [picked[n * BR:(n + 1) * BR] for n in range(NB)]
    line = jnp.concatenate(fields, axis=1).astype(jnp.bfloat16)
    row = lax.broadcasted_iota(jnp.int32, (BR, BLK), 0)
    lane = lax.broadcasted_iota(jnp.int32, (BLK, BLK), 1)
    by_matrix = jnp.zeros((BR, BLK), jnp.float32)
    by_vector = jnp.zeros((BLK, BLK), jnp.float32)

    def matrix_unit(r, total):
        block = jnp.concatenate([blocks_ref[r:r + 2, n].reshape(2 * BLK, BLK) for n in range(NB)], axis=1)
        pair = lax.dot_general(line, block, (((1,), (1,)), ((), ())), preferred_element_type=jnp.float32)
        return jnp.where(row == r, pair[:, :BLK], jnp.where(row == r + 1, pair[:, BLK:], total))

    def vector_unit(r, total):
        acc = None
        for n in range(NB):
            term = blocks_ref[r, n].astype(jnp.float32) * fields[n][r:r + 1]
            acc = term if acc is None else acc + term
        return jnp.where(lane == r, jnp.sum(acc, axis=1, keepdims=True), total)

    pairs, singles = list(range(0, MATRIX_ROWS, 2)), list(range(MATRIX_ROWS, BR))
    while pairs or singles:
        if pairs:
            by_matrix = matrix_unit(pairs.pop(0), by_matrix)
        if singles:
            by_vector = vector_unit(singles.pop(0), by_vector)
    image = jnp.where(row < MATRIX_ROWS, by_matrix, by_vector.T[:BR])
    return image - shifts_ref[0:1, k:k + 1] * v_ref[0:BR, :]


def touch_kernel(*refs):
    refs[-1][...] = jnp.zeros((S, BLK), jnp.float32)


def spread_kernel(both_ref, _, out_ref):
    both = both_ref[...].astype(jnp.bfloat16)
    for i in range(PEERS):
        out_ref[i] = both


def first_kernel(pool_ref, columns_ref, blocks_ref, v_ref, shifts_ref, out_ref, rounded_ref, hot_ref):
    wide = jnp.zeros((1, BLK - BR), jnp.int32)
    hot_ref[...] = one_hot([jnp.concatenate([columns_ref[n], wide], axis=1) for n in range(NB)])
    step_kernel(0, pool_ref, hot_ref, blocks_ref, v_ref, shifts_ref, out_ref, rounded_ref)


def step_kernel(k, pool_ref, hot_ref, blocks_ref, v_ref, shifts_ref, out_ref, rounded_ref):
    new = product(k, pool_ref, hot_ref, blocks_ref, v_ref, shifts_ref)
    out_ref[...] = new
    rounded_ref[...] = new.astype(jnp.bfloat16)


def inner(v, others):
    sub = lax.broadcasted_iota(jnp.int32, (S, BLK), 0)
    stack = jnp.zeros((S, BLK), jnp.float32)
    for j, w in enumerate(others):
        stack = jnp.where(sub == j, jnp.sum(v * w, axis=0, keepdims=True), stack)
    return jnp.sum(stack, axis=1, keepdims=True)


def last_kernel(pool_ref, hot_ref, blocks_ref, shifts_ref, *refs):
    ins, out_ref, gram_ref = refs[:S], refs[S], refs[S + 1]
    new = product(S - 1, pool_ref, hot_ref, blocks_ref, ins[-1], shifts_ref)
    out_ref[...] = new
    vectors = [ref[0:BR, :] for ref in ins] + [new]
    lane = lax.broadcasted_iota(jnp.int32, (S, BLK), 1) - GAP * lax.broadcasted_iota(jnp.int32, (S, BLK), 0)
    tile = jnp.zeros((S, BLK), jnp.float32)
    for i in range(S1):
        count = min(i + 1, S)
        tile = jnp.where((lane == i), inner(vectors[i], vectors[:count]), tile)
    row = jnp.sum(tile, axis=0, keepdims=True)
    place = lax.broadcasted_iota(jnp.int32, (1, BLK), 1)
    corner = jnp.sum(jnp.sum(new * new, axis=0, keepdims=True), axis=1, keepdims=True)
    gram_ref[...] = jnp.where(place == S1, corner, row)


def factor_kernel(rows_total, parts_ref, *refs):
    out_ref, basis_ref = refs[S1], refs[S1 + 1]
    for i in range(S1):
        basis_ref[i] = refs[i][0:BR, :]
    tile = jnp.broadcast_to(jnp.sum(parts_ref[...], axis=0) / rows_total, (S, BLK))

    def spread_lane(p):
        return jnp.broadcast_to(tile[:, p:p + 1], (S, BLK))

    a = {(j, i): spread_lane(GAP * j + i) for i in range(S1) for j in range(min(i + 1, S))}
    a[S, S] = spread_lane(S1)
    sub = lax.broadcasted_iota(jnp.int32, (S, BLK), 0)
    lane = lax.broadcasted_iota(jnp.int32, (S, BLK), 1)
    top = jnp.zeros((S, BLK), jnp.float32)
    bottom = None
    for k in range(S1):
        scale = lax.rsqrt(a[k, k])
        r = [a[k, i] * scale for i in range(k, S1)]
        whole = jnp.zeros((S, BLK), jnp.float32)
        for i in range(k, S1):
            whole = jnp.where(lane == i, r[i - k], whole)
            for j in range(k + 1, i + 1):
                a[j, i] = a[j, i] - r[j - k] * r[i - k]
        if k < S:
            top = jnp.where(sub == k, whole, top)
        else:
            bottom = whole
    out_ref[0:S, :] = top[:, 0:S1]
    out_ref[S:S1, :] = bottom[0:1, 0:S1]


def shape(*dims, dtype=jnp.float32):
    return jax.ShapeDtypeStruct(dims, dtype)


def touch(*arrays):
    return pl.pallas_call(
        touch_kernel,
        out_shape=shape(S, BLK),
        in_specs=[pl.BlockSpec(memory_space=pl.ANY)] * len(arrays),
        out_specs=VMEM,
        compiler_params=pltpu.CompilerParams(vmem_limit_bytes=58 * 1024 * 1024),
        name="touch",
    )(*arrays)


def spread(both, token):
    return pl.pallas_call(
        spread_kernel,
        out_shape=shape(PEERS, NCORE, BR, BLK, dtype=jnp.bfloat16),
        in_specs=[VMEM, pl.BlockSpec(memory_space=pl.ANY)],
        out_specs=VMEM,
        compiler_params=PARAMS,
        name="spread",
    )(both, token)


def first_step(pool, columns, blocks, v, shifts):
    return pl.pallas_call(
        first_kernel,
        out_shape=(
            shape(BR, BLK),
            shape(BR, BLK, dtype=jnp.bfloat16),
            shape(NB * BR, POOL, dtype=jnp.bfloat16),
        ),
        in_specs=[VMEM] * 5,
        out_specs=(VMEM,) * 3,
        compiler_params=PARAMS,
        name="first",
    )(pool, columns, blocks, v, shifts)


def step(k, pool, hot, blocks, v, shifts):
    return pl.pallas_call(
        functools.partial(step_kernel, k),
        out_shape=(shape(BR, BLK), shape(BR, BLK, dtype=jnp.bfloat16)),
        in_specs=[VMEM] * 5,
        out_specs=(VMEM, VMEM),
        compiler_params=PARAMS,
        name="step",
    )(pool, hot, blocks, v, shifts)


def last_step(pool, hot, blocks, shifts, vectors):
    return pl.pallas_call(
        last_kernel,
        out_shape=(shape(BR, BLK), shape(1, BLK)),
        in_specs=[VMEM] * (4 + S),
        out_specs=(VMEM, VMEM),
        compiler_params=PARAMS,
        name="last",
    )(pool, hot, blocks, shifts, *vectors)


def to_all(value, axes, peers):
    return lax.all_to_all(jnp.broadcast_to(value, (peers,) + value.shape), axes, 0, 0)


def on_device(groups, start_vector, blocks, columns, shifts):
    blocks = blocks[0, 0]
    columns = columns[0].transpose(2, 0, 1)
    shifts = shifts.reshape(1, S)
    v = start_vector[0, 0]
    vectors = [v]
    both = lax.all_gather(v, "core")
    chip = spread(both, touch(v, blocks, columns, shifts))
    for k in range(S):
        if k > 0:
            chip = lax.all_gather(rounded, "core")
            chip = jnp.broadcast_to(chip, (PEERS,) + chip.shape)
        pool = lax.all_to_all(chip, ALL, 0, 0, axis_index_groups=groups)
        if k == 0:
            v, rounded, hot = first_step(pool, columns, blocks, v, shifts)
        elif k < S - 1:
            v, rounded = step(k, pool, hot, blocks, v, shifts)
        if k < S - 1:
            vectors.append(v)
    v, gram = last_step(pool, hot, blocks, shifts, vectors)
    gram = jnp.sum(to_all(gram, ("y", "sub"), NY * SUBS), axis=0)
    parts = to_all(gram, ("z", "core"), NZ * NCORE)
    factor, basis = pl.pallas_call(
        functools.partial(factor_kernel, DOMS * SUBS * BR * BLK),
        out_shape=(shape(S1, S1), shape(S1, BR, BLK)),
        in_specs=[VMEM] * (S1 + 1),
        out_specs=(VMEM, VMEM),
        compiler_params=PARAMS,
        name="factor",
    )(parts, *vectors, v)
    return basis.reshape(S1, 1, 1, BR, BLK), factor


def solution(mesh):
    split = Mesh(mesh.devices.reshape(NY, NZ, NCORE, SUBS), ALL)
    return jax.shard_map(
        functools.partial(on_device, outer_groups()),
        mesh=split,
        in_specs=(P(DOM, "sub"), P(DOM, "sub"), P(DOM, "sub"), P()),
        out_specs=(P(None, DOM, "sub"), P()),
        check_vma=False,
    )
```
